128 devices in a mesh: pipe: 4 (over x_lo, core), dp: 4 (over z), tensor: 8 (over x_hi, y).
Axes of the slice: x: 4 (x_hi: 2, x_lo: 2; x = x_hi * 2 + x_lo), y: 4, z: 4, core: 2. Of those that a mesh axis runs over, the one named last changes fastest.
Arguments:
- hidden_in: bfloat16 [4, 4096, 8192], P('pipe', ('dp', 'tensor')), may hold values from -6 to 6
- norm_gain: bfloat16 [4, 8192], P('pipe'), may hold values from 0.5 to 1.5
- qkv_weight: bfloat16 [4, 8192, 6144], P('pipe', None, 'tensor'), may hold values from -0.0625 to 0.0625
- qkv_grad: bfloat16 [4, 4096, 6144], P('pipe', 'dp', 'tensor'), may hold values from -0.3984375 to 0.3984375
- upper_grad: bfloat16 [4, 4096, 8192], P('pipe', ('dp', 'tensor')), may hold values from -0.59765625 to 0.59765625
Outputs:
- weight_grad: bfloat16 [4, 8192, 6144], P('pipe', 'dp', 'tensor')
- input_grad: bfloat16 [4, 4096, 8192], P('pipe', ('dp', 'tensor'))
The draws below stay inside these ranges and needn't reach their ends.
All inputs are finite; a program needn't handle non-finite values.
Results may differ from the reference program's by a relative error of at most 0.013.
Values may be sent and summed in bfloat16 or wider, within the bound.
No kernel may reach another device: no remote copies, remote signals or barrier semaphores. Data moves between devices by JAX's collectives and lax.ppermute only.
A program may use at most 128 MiB of HBM per device.

```python
import jax
import jax.numpy as jnp
from jax import lax

D = 8192
COLS = 6144
SEQ = 1024
TOKENS = 4096
N_PIPE = 4
N_DP = 4
N_TENSOR = 8


def block_levels(rng, shape, split, smallest, top_value):
    level = 1.0
    for axis_at, shards_of in split:
        draws = jax.random.uniform(jax.random.fold_in(jax.random.fold_in(rng, 6), axis_at), (shards_of,), jnp.float32, smallest / len(split), top_value / len(split))
        level = level * jnp.repeat(jnp.exp(draws), shape[axis_at] // shards_of).reshape((-1,) + (1,) * (len(shape) - 1 - axis_at))
    return level


def scatter_about(rng, extent, deviation, most, shards=(), held_as=jnp.bfloat16):
    array = deviation * jax.random.normal(rng, extent, jnp.float32)
    if shards:
        array = array * block_levels(rng, extent, shards, -0.22, 0.18)
    return jnp.clip(array, -most, most).astype(held_as)


def setup_inputs(seed: int = 0) -> dict:
    streams_of = jax.random.split(jax.random.key(seed), 6)
    hidden_in = scatter_about(streams_of[0], (N_PIPE, TOKENS, D), 1.0, 6.0, ((0, 4), (1, 32)))
    norm_gain = jnp.clip(1.0 + 0.1 * jax.random.normal(streams_of[1], (N_PIPE, D), jnp.float32), 0.5, 1.5).astype(jnp.bfloat16)
    qkv_weight = scatter_about(streams_of[2], (N_PIPE, D, COLS), D ** -0.5, 0.0625, ((0, 4), (2, 8)))
    qkv_grad = scatter_about(streams_of[3], (N_PIPE, TOKENS, COLS), 0.0625, 0.3984375, ((0, 4), (1, 4), (2, 8)))
    upper_grad = scatter_about(streams_of[4], (N_PIPE, TOKENS, D), 0.1, 0.59765625, ((0, 4), (1, 32)))
    return dict(hidden_in=hidden_in, norm_gain=norm_gain, qkv_weight=qkv_weight, qkv_grad=qkv_grad, upper_grad=upper_grad)


def round_trip(value):
    low = lax.optimization_barrier(value.astype(jnp.bfloat16))
    return low.astype(jnp.float32)

def reference(hidden_in, norm_gain, qkv_weight, qkv_grad, upper_grad):
    block = COLS // N_TENSOR
    weight_list = []
    input_list = []
    for layer in range(N_PIPE):
        input_rows = hidden_in[layer].astype(jnp.float32)
        scale_factor = norm_gain[layer].astype(jnp.float32)
        inverse_deviation = lax.rsqrt(lax.optimization_barrier(jnp.mean(input_rows * input_rows, axis=-1, keepdims=True)) + 1e-06)
        centered_input = input_rows * inverse_deviation
        normed_input = (centered_input * scale_factor).astype(jnp.bfloat16)
        grads = qkv_grad[layer]
        weight = qkv_weight[layer]
        total = jnp.zeros((D, COLS), jnp.float32)
        for member in range(N_DP):
            rows = normed_input[member * SEQ:(member + 1) * SEQ]
            part = lax.dot_general(rows, grads[member * SEQ:(member + 1) * SEQ], (((0,), (0,)), ((), ())), preferred_element_type=jnp.float32)
            total = total + round_trip(part)
        weight_list.append(total.astype(jnp.bfloat16))
        hidden_grad = jnp.zeros((TOKENS, D), jnp.float32)
        for column in range(N_TENSOR):
            part = lax.dot_general(grads[:, column * block:(column + 1) * block], weight[:, column * block:(column + 1) * block], (((1,), (1,)), ((), ())), preferred_element_type=jnp.float32)
            hidden_grad = hidden_grad + round_trip(part)
        if layer + 1 < N_PIPE:
            received_gradient = upper_grad[layer + 1].astype(jnp.float32)
        else:
            received_gradient = jnp.zeros((TOKENS, D), jnp.float32)
        scaled_gradient = scale_factor * hidden_grad
        inner_product = lax.optimization_barrier(jnp.mean(scaled_gradient * centered_input, axis=-1, keepdims=True))
        final_output = received_gradient + inverse_deviation * (scaled_gradient - centered_input * inner_product)
        input_list.append(final_output.astype(jnp.bfloat16))
    return (jnp.stack(weight_list), jnp.stack(input_list))
```

```python
import jax
import jax.numpy as jnp
from jax import lax
from jax.sharding import PartitionSpec as P

N_Z = 4
N_Y = 4
F32 = jnp.float32
BF16 = jnp.bfloat16


def from_z(block, o):
    return lax.ppermute(block, "dp", [((i + o) % N_Z, i) for i in range(N_Z)])


def from_y(block, o):
    return lax.ppermute(
        block,
        "tensor",
        [(x * N_Y + (i + o) % N_Y, x * N_Y + i) for x in range(2) for i in range(N_Y)],
    )


def from_x(block):
    return lax.ppermute(block, "tensor", [(i, (i + N_Y) % (2 * N_Y)) for i in range(2 * N_Y)])


def dot_nt(a, b):
    return lax.dot_general(a, b, (((1,), (1,)), ((), ())), preferred_element_type=F32)


def dot_tn(a, b):
    return lax.dot_general(a, b, (((0,), (0,)), ((), ())), preferred_element_type=F32)


def shards(hidden_in, norm_gain, qkv_weight, qkv_grad, upper_grad):
    place = lax.axis_index("tensor")
    xh, y, z = place // N_Y, place % N_Y, lax.axis_index("dp")
    rows = hidden_in.shape[1]
    width = hidden_in.shape[2]
    part = width // N_Z
    half = part // 2
    cols = qkv_grad.shape[2]
    layers = lax.axis_size("pipe")

    grads = qkv_grad[0].reshape(2, N_Y, rows, cols)

    def turned(which):
        side = lax.dynamic_index_in_dim(grads, which, 0, keepdims=False)
        return jnp.concatenate(
            [lax.dynamic_slice_in_dim(side, (y + q) % N_Y, 1, 0) for q in range(N_Y)], 0
        )

    partner = from_x(turned(1 - xh))
    g_own = jnp.concatenate([turned(xh), partner], -1)
    weight = lax.dynamic_slice_in_dim(qkv_weight[0], z * part, part, 0)
    w_both = jnp.concatenate([weight, from_x(weight)], 1)
    received_gradient = lax.ppermute(upper_grad, "pipe", [(i + 1, i) for i in range(layers - 1)])

    input_rows = hidden_in[0].astype(F32)
    scale_factor = norm_gain[0].astype(F32)
    inverse_deviation = lax.rsqrt(jnp.mean(input_rows * input_rows, axis=-1, keepdims=True) + 1e-06)

    def normed(block):
        at = (block % N_Z) * part
        x = lax.dynamic_slice_in_dim(hidden_in[0], at, part, 1).astype(F32)
        s = lax.dynamic_slice_in_dim(norm_gain[0], at, part, 0).astype(F32)
        return ((x * inverse_deviation) * s).astype(BF16)

    n_far = jnp.concatenate([from_z(normed(z - o), o) for o in (1, 3, 2)], 0)
    n_near = normed(z)

    def gather_y(block):
        up, down = from_y(block, 1), from_y(block, 3)
        cut = block.shape[0] // 2
        across = jnp.concatenate([from_y(up[:cut], 1), from_y(down[cut:], 3)], 0)
        return [block, up, across, down]

    near, far = gather_y(n_near), gather_y(n_far)

    g_up, g_down = from_z(g_own, 1), from_z(g_own, 3)
    g_across = jnp.concatenate([from_z(g_up[:2], 1), from_z(g_down[2:], 3)], 0)
    g_all = jnp.stack([g_up, g_down, g_across, g_own], 1)

    def summed(first, last):
        count = last - first

        def partial(q):
            return dot_nt(g_all[q, first:last].reshape(count * rows, 2 * cols), w_both)

        p2 = partial(2).astype(BF16)
        first_hop_up = from_y(p2[:, :half], 3)
        first_hop_down = from_y(p2[:, half:], 1)
        p1, p3 = partial(1), partial(3)
        up_own = from_y(p1[:, half:].astype(BF16), 3)
        down_own = from_y(p3[:, :half].astype(BF16), 1)
        up_sum = from_y((p1[:, :half] + first_hop_up.astype(F32)).astype(BF16), 3)
        down_sum = from_y((p3[:, half:] + first_hop_down.astype(F32)).astype(BF16), 1)
        p0 = partial(0)
        left = p0[:, :half] + up_sum.astype(F32) + down_own.astype(F32)
        right = p0[:, half:] + down_sum.astype(F32) + up_own.astype(F32)
        return jnp.concatenate([left, right], 1).astype(BF16).reshape(count, rows, part)

    h_far = summed(0, 3)
    h_near = summed(3, 4)
    h1 = from_z(h_far[1], 1)
    h3 = from_z(h_far[0], 3)
    h2 = from_z(h_far[2], 2)
    turned_h = jnp.stack([h_near[0], h1, h2, h3], 0)
    hidden_grad = jnp.concatenate(
        [
            lax.dynamic_index_in_dim(turned_h, (b - z) % N_Z, 0, keepdims=False)
            for b in range(N_Z)
        ],
        1,
    ).astype(F32)

    n_all = jnp.concatenate([jnp.concatenate([far[q], near[q]], 0) for q in range(N_Y)], 0)
    g_flat = g_all.reshape(N_Y * N_Z * rows, 2 * cols)
    dw_partner = dot_tn(n_all, g_flat[:, cols:]).astype(BF16)
    dw_got = from_x(dw_partner)
    weight_out = (dot_tn(n_all, g_flat[:, :cols]) + dw_got.astype(F32)).astype(BF16)

    centered_input = input_rows * inverse_deviation
    scaled_gradient = scale_factor * hidden_grad
    inner_product = jnp.mean(scaled_gradient * centered_input, axis=-1, keepdims=True)
    final_output = received_gradient[0].astype(F32) + inverse_deviation * (
        scaled_gradient - centered_input * inner_product
    )
    return (weight_out[None], final_output.astype(BF16)[None])


def solution(mesh):
    placed = (
        P("pipe", ("dp", "tensor"), None),
        P("pipe", None),
        P("pipe", None, "tensor"),
        P("pipe", "dp", "tensor"),
        P("pipe", ("dp", "tensor"), None),
    )
    return jax.shard_map(
        shards,
        mesh=mesh,
        in_specs=placed,
        out_specs=(P("pipe", "dp", "tensor"), P("pipe", ("dp", "tensor"), None)),
        check_vma=False,
    )
```

```python
import functools

import jax
import jax.numpy as jnp
from jax import lax
from jax.experimental import pallas as pl
from jax.experimental.pallas import tpu as pltpu
from jax.sharding import PartitionSpec as P

N_Z = 4
N_Y = 4
F32 = jnp.float32
BF16 = jnp.bfloat16
VMEM_BYTES = 40 * 2**20


class Chains:
    def __init__(self):
        self.last = {}

    def __call__(self, key, block, send):
        if key in self.last:
            block, _ = lax.optimization_barrier((block, self.last[key]))
        self.last[key] = send(block)
        return self.last[key]


def from_z(block, o):
    return lax.ppermute(block, "dp", [((i + o) % N_Z, i) for i in range(N_Z)])


def from_y(block, o):
    return lax.ppermute(
        block,
        "tensor",
        [(x * N_Y + (i + o) % N_Y, x * N_Y + i) for x in range(2) for i in range(N_Y)],
    )


def from_x(block):
    return lax.ppermute(block, "tensor", [(i, (i + N_Y) % (2 * N_Y)) for i in range(2 * N_Y)])


def dot_nt(a, b):
    return lax.dot_general(a, b, (((1,), (1,)), ((), ())), preferred_element_type=F32)


def dot_nn(a, b):
    return lax.dot_general(a, b, (((1,), (0,)), ((), ())), preferred_element_type=F32)


def call(kernel, grid, in_specs, out_specs, out_shape, flops=0, bytes_accessed=0, name=None):
    return pl.pallas_call(
        kernel,
        grid=grid,
        in_specs=in_specs,
        out_specs=out_specs,
        out_shape=out_shape,
        name=name,
        compiler_params=pltpu.CompilerParams(vmem_limit_bytes=VMEM_BYTES),
        cost_estimate=pl.CostEstimate(
            flops=flops, bytes_accessed=bytes_accessed, transcendentals=0
        ),
    )


SMEM = pl.BlockSpec(memory_space=pltpu.SMEM)
WHOLE = pl.BlockSpec(memory_space=pltpu.VMEM)


def normalize(z, hidden, gain):
    rows, width = hidden.shape
    part = width // N_Z

    def kernel(z_ref, h_ref, g_ref, r_ref, *out_refs):
        x = h_ref[...].astype(F32)
        r = lax.rsqrt(jnp.mean(x * x, axis=-1, keepdims=True) + 1e-06)
        r_ref[...] = jnp.broadcast_to(r, r_ref.shape)
        for d in range(N_Z):
            at = pl.multiple_of(lax.rem(z_ref[0] + d, N_Z) * part, part)
            x = h_ref[:, pl.ds(at, part)].astype(F32)
            g = g_ref[:, pl.ds(at, part)].astype(F32)
            out_refs[d][...] = ((x * r) * g).T.astype(BF16)

    return call(
        kernel,
        (),
        [SMEM, WHOLE, WHOLE],
        [WHOLE] * (1 + N_Z),
        [jax.ShapeDtypeStruct((rows, 128), F32)]
        + [jax.ShapeDtypeStruct((part, rows), BF16)] * N_Z,
        bytes_accessed=4 * rows * width,
        name="normalize",
    )(z, hidden, gain)


def partial_sums(jobs, g_own, g_par, w_own, w_par, extras, per_sequence=False):
    _, rows, cols = g_own[0].shape
    part = w_own.shape[0]
    half = part // 2
    step = 256
    steps = half // step
    qs = sorted({q for q, _, _ in jobs})
    sides = sorted({side for _, side, _ in jobs})
    n_g, n_w, n_e = 2 * N_Z * len(qs), 2 * len(sides), len(extras)

    def kernel(*refs):
        g_refs, w_refs = refs[:n_g], refs[n_g : n_g + n_w]
        e_refs, outs = refs[n_g + n_w : n_g + n_w + n_e], refs[n_g + n_w + n_e :]
        for k, (q, side, adds) in enumerate(jobs):
            at = qs.index(q) * 2 * N_Z
            left = jnp.concatenate([g_refs[at + o][0] for o in range(N_Z)], 0)
            right = jnp.concatenate([g_refs[at + N_Z + o][0] for o in range(N_Z)], 0)
            s = sides.index(side) * 2
            total = dot_nt(left, w_refs[s][...]) + dot_nt(right, w_refs[s + 1][...])
            total = total.reshape(N_Z, rows, step)
            for e in adds:
                total = total + e_refs[e][...].astype(F32)
            if per_sequence:
                for o in range(N_Z):
                    outs[o][side] = total[o].astype(BF16)
            else:
                outs[k][...] = total.astype(BF16)

    in_specs, operands = [], []
    for q in qs:
        for arrays in (g_own, g_par):
            for o in range(N_Z):
                in_specs.append(pl.BlockSpec((1, rows, cols), functools.partial(lambda q, i: (q, 0, 0), q)))
                operands.append(arrays[o])
    for side in sides:
        for w in (w_own, w_par):
            in_specs.append(
                pl.BlockSpec((step, cols), functools.partial(lambda s, i: (s * steps + i, 0), side))
            )
            operands.append(w)
    chunk = pl.BlockSpec((N_Z, rows, step), lambda i: (0, 0, i))
    in_specs += [chunk] * n_e
    operands += list(extras)
    if per_sequence:
        out_specs = [pl.BlockSpec((2, rows, step), lambda i: (0, 0, i))] * N_Z
        out_shape = [jax.ShapeDtypeStruct((2, rows, half), BF16)] * N_Z
    else:
        out_specs = [chunk] * len(jobs)
        out_shape = [jax.ShapeDtypeStruct((N_Z, rows, half), BF16)] * len(jobs)
    return call(
        kernel, (steps,), in_specs, out_specs, out_shape, name="partial_sums"
    )(*operands)


def weight_terms(n_pieces, g):
    part, rows = n_pieces[0][0].shape
    cols = g[0].shape[2]
    step = 256

    def kernel(*refs):
        n_refs, g_refs, out_ref = refs[: N_Z * N_Y], refs[N_Z * N_Y : -1], refs[-1]
        total = None
        for o in range(N_Z):
            left = jnp.concatenate([n_refs[o * N_Y + q][...] for q in range(N_Y)], 1)
            term = dot_nn(left, g_refs[o][...].reshape(N_Y * rows, cols))
            total = term if total is None else total + term
        out_ref[...] = total.astype(BF16)

    return call(
        kernel,
        (part // step,),
        [pl.BlockSpec((step, rows), lambda i: (i, 0))] * (N_Z * N_Y)
        + [pl.BlockSpec((N_Y, rows, cols), lambda i: (0, 0, 0))] * N_Z,
        pl.BlockSpec((step, cols), lambda i: (i, 0)),
        jax.ShapeDtypeStruct((part, cols), BF16),
        name="weight_terms",
    )(*[n_pieces[o][q] for o in range(N_Z) for q in range(N_Y)], *g)


def finish(z, deviation, gain, hidden, received, h):
    rows, width = hidden.shape
    part = width // N_Z
    half = part // 2
    step = 32

    def kernel(z_ref, r_ref, g_ref, x_ref, u_ref, *refs):
        h_refs, out_ref = refs[:-1], refs[-1]
        r = r_ref[:, :1]
        spots = [
            (o, s, pl.multiple_of(lax.rem(z_ref[0] + o, N_Z) * part + s * half, half))
            for o in range(N_Z)
            for s in range(2)
        ]

        def terms(o, s, at):
            xhat = x_ref[:, pl.ds(at, half)].astype(F32) * r
            scaled = g_ref[:, pl.ds(at, half)].astype(F32) * h_refs[o][s].astype(F32)
            return xhat, scaled

        total = jnp.zeros((step, 1), F32)
        for spot in spots:
            xhat, scaled = terms(*spot)
            total += jnp.sum(scaled * xhat, axis=-1, keepdims=True)
        mean = total / width
        for spot in spots:
            xhat, scaled = terms(*spot)
            at = spot[2]
            up = u_ref[0, :, pl.ds(at, half)].astype(F32)
            out_ref[0, :, pl.ds(at, half)] = (up + r * (scaled - xhat * mean)).astype(BF16)

    return call(
        kernel,
        (rows // step,),
        [
            SMEM,
            pl.BlockSpec((step, 128), lambda i: (i, 0)),
            pl.BlockSpec((1, width), lambda i: (0, 0)),
            pl.BlockSpec((step, width), lambda i: (i, 0)),
            pl.BlockSpec((1, step, width), lambda i: (0, i, 0)),
        ]
        + [pl.BlockSpec((2, step, half), lambda i: (0, i, 0))] * N_Z,
        pl.BlockSpec((1, step, width), lambda i: (0, i, 0)),
        jax.ShapeDtypeStruct((1, rows, width), BF16),
        name="finish",
    )(z, deviation, gain, hidden, received, *h)


def shards(hidden_in, norm_gain, qkv_weight, qkv_grad, upper_grad):
    place = lax.axis_index("tensor")
    xh, y, z = place // N_Y, place % N_Y, lax.axis_index("dp")
    z_array = z.reshape(1).astype(jnp.int32)
    rows = hidden_in.shape[1]
    part = hidden_in.shape[2] // N_Z
    cols = qkv_grad.shape[2]
    layers = lax.axis_size("pipe")

    chains = Chains()

    def zz(block, o):
        return chains("z%d" % o, block, lambda b: from_z(b, o))

    def yy(block, o):
        return chains("y%d" % o, block, lambda b: from_y(b, o))

    def xx(block):
        return chains("x", block, from_x)

    grads = qkv_grad[0].reshape(2, N_Y, rows, cols)

    def turned(which):
        side = lax.dynamic_index_in_dim(grads, which, 0, keepdims=False)
        return jnp.concatenate(
            [lax.dynamic_slice_in_dim(side, (y + q) % N_Y, 1, 0) for q in range(N_Y)], 0
        )

    par0 = xx(turned(1 - xh))
    own0 = turned(xh)
    w_own = lax.dynamic_slice_in_dim(qkv_weight[0], z * part, part, 0)
    w_par = xx(w_own)
    received = lax.ppermute(upper_grad, "pipe", [(i + 1, i) for i in range(layers - 1)])

    deviation, *n_to = normalize(z_array, hidden_in[0], norm_gain)
    n_near = [n_to[0], zz(n_to[3], 1), zz(n_to[2], 2), zz(n_to[1], 3)]

    n_pieces = []
    for o, piece in enumerate(n_near):
        up, down = yy(piece, 1), yy(piece, 3)
        across = yy(up, 1) if o in (0, 1) else yy(down, 3)
        n_pieces.append([piece, up, across, down])

    own1, own3 = zz(own0, 1), zz(own0, 3)
    own2 = zz(own1, 1)
    par1, par3 = zz(par0, 1), zz(par0, 3)
    par2 = zz(par3, 3)
    g_own, g_par = [own0, own1, own2, own3], [par0, par1, par2, par3]

    sums = functools.partial(partial_sums, g_own=g_own, g_par=g_par, w_own=w_own, w_par=w_par)
    p2a, p2b = sums([(2, 0, ()), (2, 1, ())], extras=[])
    hop_up, hop_down = yy(p2a, 3), yy(p2b, 1)
    p1b, p3a = sums([(1, 1, ()), (3, 0, ())], extras=[])
    up_b, down_a = yy(p1b, 3), yy(p3a, 1)
    p1a, p3b = sums([(1, 0, (0,)), (3, 1, (1,))], extras=[hop_up, hop_down])
    up_a, down_b = yy(p1a, 3), yy(p3b, 1)
    h_to = sums(
        [(0, 0, (0, 1)), (0, 1, (2, 3))],
        extras=[up_a, down_a, down_b, up_b],
        per_sequence=True,
    )
    h = [h_to[0], zz(h_to[3], 1), zz(h_to[2], 2), zz(h_to[1], 3)]

    dw_got = xx(weight_terms(n_pieces, g_par))
    dw_own = weight_terms(n_pieces, g_own)
    weight_out = (dw_own.astype(F32) + dw_got.astype(F32)).astype(BF16)

    input_out = finish(z_array, deviation, norm_gain, hidden_in[0], received, h)
    return (weight_out[None], input_out)


def solution(mesh):
    placed = (
        P("pipe", ("dp", "tensor"), None),
        P("pipe", None),
        P("pipe", None, "tensor"),
        P("pipe", "dp", "tensor"),
        P("pipe", ("dp", "tensor"), None),
    )
    return jax.shard_map(
        shards,
        mesh=mesh,
        in_specs=placed,
        out_specs=(P("pipe", "dp", "tensor"), P("pipe", ("dp", "tensor"), None)),
        check_vma=False,
    )
```

```python
import functools

import jax
import jax.numpy as jnp
from jax import lax
from jax.experimental import pallas as pl
from jax.experimental.pallas import tpu as pltpu
from jax.sharding import PartitionSpec as P

N_Z = 4
N_Y = 4
F32 = jnp.float32
BF16 = jnp.bfloat16
VMEM_BYTES = 20 * 2**20


class Chains:
    def __init__(self):
        self.last = {}

    def __call__(self, key, block, send):
        block = self.after(block, key)
        self.last[key] = send(block)
        return self.last[key]

    def after(self, block, *keys):
        for key in keys:
            if key in self.last:
                block, _ = lax.optimization_barrier((block, self.last[key]))
        return block


def from_z(block, o):
    return lax.ppermute(block, "dp", [((i + o) % N_Z, i) for i in range(N_Z)])


def from_y(block, o):
    return lax.ppermute(
        block,
        "tensor",
        [(x * N_Y + (i + o) % N_Y, x * N_Y + i) for x in range(2) for i in range(N_Y)],
    )


def from_x(block):
    return lax.ppermute(block, "tensor", [(i, (i + N_Y) % (2 * N_Y)) for i in range(2 * N_Y)])


def dot_nt(a, b):
    return lax.dot_general(a, b, (((1,), (1,)), ((), ())), preferred_element_type=F32)


def dot_nn(a, b):
    return lax.dot_general(a, b, (((1,), (0,)), ((), ())), preferred_element_type=F32)


def call(kernel, grid, in_specs, out_specs, out_shape, flops=0, bytes_accessed=0, name=None):
    return pl.pallas_call(
        kernel,
        grid_spec=pltpu.PrefetchScalarGridSpec(
            num_scalar_prefetch=1, grid=grid, in_specs=in_specs, out_specs=out_specs
        ),
        out_shape=out_shape,
        name=name,
        compiler_params=pltpu.CompilerParams(vmem_limit_bytes=VMEM_BYTES),
        cost_estimate=pl.CostEstimate(
            flops=flops, bytes_accessed=bytes_accessed, transcendentals=0
        ),
    )


WHOLE = pl.BlockSpec(memory_space=pltpu.VMEM)


def normalize(place, hidden, gain):
    rows, width = hidden.shape
    part = width // N_Z

    def kernel(at_ref, h_ref, g_ref, r_ref, *out_refs):
        x = h_ref[...].astype(F32)
        r = lax.rsqrt(jnp.mean(x * x, axis=-1, keepdims=True) + 1e-06)
        r_ref[...] = jnp.broadcast_to(r, r_ref.shape)
        for d in range(N_Z):
            at = pl.multiple_of(lax.rem(at_ref[0] + d, N_Z) * part, part)
            x = h_ref[:, pl.ds(at, part)].astype(F32)
            g = g_ref[:, pl.ds(at, part)].astype(F32)
            out_refs[d][...] = ((x * r) * g).T.astype(BF16)

    return call(
        kernel,
        (),
        [WHOLE, WHOLE],
        [WHOLE] * (1 + N_Z),
        [jax.ShapeDtypeStruct((rows, 128), F32)]
        + [jax.ShapeDtypeStruct((part, rows), BF16)] * N_Z,
        bytes_accessed=4 * rows * width,
        name="normalize",
    )(place, hidden, gain)


def partial_sums(place, seqs, jobs, g_own, g_par, w_own, w_par, extras=(), per_sequence=False):
    _, rows, cols = g_own[0].shape
    part = w_own.shape[0]
    half = part // 2
    step = 256
    steps = half // step
    count = len(seqs)
    qs = sorted({q for q, _, _ in jobs})
    sides = sorted({side for _, side, _ in jobs})
    n_g, n_w, n_e = 2 * count * len(qs), 2 * len(sides), len(extras)

    def kernel(at_ref, *refs):
        g_refs, w_refs = refs[:n_g], refs[n_g : n_g + n_w]
        e_refs, outs = refs[n_g + n_w : n_g + n_w + n_e], refs[n_g + n_w + n_e :]
        for k, (q, side, adds) in enumerate(jobs):
            at = qs.index(q) * 2 * count
            left = jnp.concatenate([g_refs[at + o][0] for o in range(count)], 0)
            right = jnp.concatenate([g_refs[at + count + o][0] for o in range(count)], 0)
            s = sides.index(side) * 2
            total = dot_nt(left, w_refs[s][...]) + dot_nt(right, w_refs[s + 1][...])
            total = total.reshape(count, rows, step)
            for e in adds:
                total = total + e_refs[e][...].astype(F32)
            if per_sequence:
                for o in range(count):
                    outs[o][side] = total[o].astype(BF16)
            else:
                outs[k][...] = total.astype(BF16)

    def tokens_of(q):
        return pl.BlockSpec((1, rows, cols), lambda i, at: (lax.rem(at[1] + q, N_Y), 0, 0))

    def features_of(side):
        return pl.BlockSpec((step, cols), lambda i, at: (side * steps + i, 0))

    in_specs, operands = [], []
    for q in qs:
        for arrays in (g_own, g_par):
            for o in seqs:
                in_specs.append(tokens_of(q))
                operands.append(arrays[o])
    for side in sides:
        for w in (w_own, w_par):
            in_specs.append(features_of(side))
            operands.append(w)
    chunk = pl.BlockSpec((count, rows, step), lambda i, at: (0, 0, i))
    in_specs += [chunk] * n_e
    operands += list(extras)
    if per_sequence:
        out_specs = [pl.BlockSpec((2, rows, step), lambda i, at: (0, 0, i))] * count
        out_shape = [jax.ShapeDtypeStruct((2, rows, half), BF16)] * count
    else:
        out_specs = [chunk] * len(jobs)
        out_shape = [jax.ShapeDtypeStruct((count, rows, half), BF16)] * len(jobs)
    return call(
        kernel, (steps,), in_specs, out_specs, out_shape, name="partial_sums"
    )(place, *operands)


def weight_terms(place, n_pieces, g):
    part, rows = n_pieces[0][0].shape
    cols = g[0].shape[2]
    step = 256

    def kernel(at_ref, *refs):
        n_refs, g_refs, out_ref = refs[: N_Z * N_Y], refs[N_Z * N_Y : -1], refs[-1]
        total = None
        for o in range(N_Z):
            left = jnp.concatenate([n_refs[o * N_Y + q][...] for q in range(N_Y)], 1)
            right = jnp.concatenate(
                [g_refs[o][lax.rem(at_ref[1] + q, N_Y)] for q in range(N_Y)], 0
            )
            term = dot_nn(left, right)
            total = term if total is None else total + term
        out_ref[...] = total.astype(BF16)

    return call(
        kernel,
        (part // step,),
        [pl.BlockSpec((step, rows), lambda i, at: (i, 0))] * (N_Z * N_Y)
        + [pl.BlockSpec((N_Y, rows, cols), lambda i, at: (0, 0, 0))] * N_Z,
        pl.BlockSpec((step, cols), lambda i, at: (i, 0)),
        jax.ShapeDtypeStruct((part, cols), BF16),
        name="weight_terms",
    )(place, *[n_pieces[o][q] for o in range(N_Z) for q in range(N_Y)], *g)


def finish(place, deviation, gain, hidden, received, h):
    rows, width = hidden.shape
    part = width // N_Z
    half = part // 2
    step = 32

    def kernel(at_ref, r_ref, g_ref, x_ref, u_ref, *refs):
        h_refs, out_ref = refs[:-1], refs[-1]
        r = r_ref[:, :1]
        spots = [
            (o, s, pl.multiple_of(lax.rem(at_ref[0] + o, N_Z) * part + s * half, half))
            for o in range(N_Z)
            for s in range(2)
        ]

        def terms(o, s, at):
            xhat = x_ref[:, pl.ds(at, half)].astype(F32) * r
            scaled = g_ref[:, pl.ds(at, half)].astype(F32) * h_refs[o][s].astype(F32)
            return xhat, scaled

        total = jnp.zeros((step, 1), F32)
        for spot in spots:
            xhat, scaled = terms(*spot)
            total += jnp.sum(scaled * xhat, axis=-1, keepdims=True)
        mean = total / width
        for spot in spots:
            xhat, scaled = terms(*spot)
            at = spot[2]
            up = u_ref[0, :, pl.ds(at, half)].astype(F32)
            out_ref[0, :, pl.ds(at, half)] = (up + r * (scaled - xhat * mean)).astype(BF16)

    return call(
        kernel,
        (rows // step,),
        [
            pl.BlockSpec((step, 128), lambda i, at: (i, 0)),
            pl.BlockSpec((1, width), lambda i, at: (0, 0)),
            pl.BlockSpec((step, width), lambda i, at: (i, 0)),
            pl.BlockSpec((1, step, width), lambda i, at: (0, i, 0)),
        ]
        + [pl.BlockSpec((2, step, half), lambda i, at: (0, i, 0))] * N_Z,
        pl.BlockSpec((1, step, width), lambda i, at: (0, i, 0)),
        jax.ShapeDtypeStruct((1, rows, width), BF16),
        name="finish",
    )(place, deviation, gain, hidden, received, *h)


def shards(hidden_in, norm_gain, qkv_weight, qkv_grad, upper_grad):
    tensor = lax.axis_index("tensor")
    xh, y, z = tensor // N_Y, tensor % N_Y, lax.axis_index("dp")
    place = jnp.stack([z, y]).astype(jnp.int32)
    rows = hidden_in.shape[1]
    part = hidden_in.shape[2] // N_Z
    cols = qkv_grad.shape[2]
    layers = lax.axis_size("pipe")
    chains = Chains()

    def zz(block, o):
        return chains("z%d" % o, block, lambda b: from_z(b, o))

    def yy(block, o):
        return chains("y%d" % o, block, lambda b: from_y(b, o))

    def xx(block):
        return chains("x", block, from_x)

    grads = qkv_grad[0].reshape(2, N_Y, rows, cols)
    par0 = xx(lax.dynamic_index_in_dim(grads, 1 - xh, 0, keepdims=False))
    own0 = lax.dynamic_index_in_dim(grads, xh, 0, keepdims=False)
    w_own = lax.dynamic_slice_in_dim(qkv_weight[0], z * part, part, 0)
    w_par = xx(w_own)
    received = lax.ppermute(upper_grad, "pipe", [(i + 1, i) for i in range(layers - 1)])

    deviation, *n_to = normalize(place, hidden_in[0], norm_gain)
    n1, n3 = zz(n_to[3], 1), zz(n_to[1], 3)
    chains.last["z2"] = n2 = from_z(chains.after(n_to[2], "z1", "z3"), 2)
    n_near = [n_to[0], n1, n2, n3]
    order = (0, 1, 3, 2)
    n_up, n_down = {}, {}
    for o in order:
        n_up[o], n_down[o] = yy(n_near[o], 1), yy(n_near[o], 3)
    n_across = {}
    for one, other in ((0, 1), (3, 2)):
        n_across[one], n_across[other] = yy(n_up[one], 1), yy(n_down[other], 3)
    n_pieces = [[n_near[o], n_up[o], n_across[o], n_down[o]] for o in range(N_Z)]

    own0_sent = chains.after(own0, "z2")
    own1, own3 = zz(own0_sent, 1), zz(own0_sent, 3)
    par1, par3 = zz(par0, 1), zz(par0, 3)
    own2, par2 = zz(own1, 1), zz(par3, 3)
    g_own, g_par = [own0, own1, own2, own3], [par0, par1, par2, par3]

    def summed(seqs):
        sums = functools.partial(
            partial_sums, place, seqs, g_own=g_own, g_par=g_par, w_own=w_own, w_par=w_par
        )
        p2a, p2b = sums([(2, 0, ()), (2, 1, ())])
        p2a, p2b = chains.after(p2a, "h"), chains.after(p2b, "h")
        hop_up, hop_down = yy(p2a, 3), yy(p2b, 1)
        p1b, p3a = sums([(1, 1, ()), (3, 0, ())])
        up_b, down_a = yy(p1b, 3), yy(p3a, 1)
        hop_up, hop_down = chains.after(hop_up, "h2"), chains.after(hop_down, "h2")
        p1a, p3b = sums([(1, 0, (0,)), (3, 1, (1,))], extras=[hop_up, hop_down])
        up_a, down_b = yy(p1a, 3), yy(p3b, 1)
        up_a = chains.after(up_a, "dw", "h1", "h3")
        return sums(
            [(0, 0, (0, 1)), (0, 1, (2, 3))],
            extras=[up_a, down_a, down_b, up_b],
            per_sequence=True,
        )

    dw_got = xx(weight_terms(place, n_pieces, g_par))
    chains.last["dw"] = dw_own = weight_terms(place, n_pieces, g_own)
    h_to1, h_to2, h_to3 = summed([1, 2, 3])
    h2 = chains.last["h2"] = from_z(h_to2, 2)
    h1, h3 = from_z(chains.after(h_to3, "h2"), 1), from_z(chains.after(h_to1, "h2"), 3)
    chains.last.update(h=h_to2, h1=h1, h3=h3)
    (h0,) = summed([0])

    dw_got = chains.after(dw_got, "h1", "h3")
    weight_out = (dw_own.astype(F32) + dw_got.astype(F32)).astype(BF16)

    input_out = finish(place, deviation, norm_gain, hidden_in[0], received, [h0, h1, h2, h3])
    return (weight_out[None], input_out)


def solution(mesh):
    placed = (
        P("pipe", ("dp", "tensor"), None),
        P("pipe", None),
        P("pipe", None, "tensor"),
        P("pipe", "dp", "tensor"),
        P("pipe", ("dp", "tensor"), None),
    )
    return jax.shard_map(
        shards,
        mesh=mesh,
        in_specs=placed,
        out_specs=(P("pipe", "dp", "tensor"), P("pipe", ("dp", "tensor"), None)),
        check_vma=False,
    )
```

```python
import functools

import jax
import jax.numpy as jnp
from jax import lax
from jax.experimental import pallas as pl
from jax.experimental.pallas import tpu as pltpu
from jax.sharding import PartitionSpec as P

N_Z = 4
N_Y = 4
F32 = jnp.float32
BF16 = jnp.bfloat16
VMEM_BYTES = 20 * 2**20


class Chains:
    def __init__(self):
        self.sent = {}

    def __call__(self, key, block, send, depth=1):
        sent = self.sent.setdefault(key, [])
        if len(sent) >= depth:
            block, _ = lax.optimization_barrier((block, sent[-depth]))
        sent.append(send(block))
        return sent[-1]


def after(block, *others):
    return lax.optimization_barrier((block, *others))[0]


def from_z(block, o):
    return lax.ppermute(block, "dp", [((i + o) % N_Z, i) for i in range(N_Z)])


def from_y(block, o):
    return lax.ppermute(
        block,
        "tensor",
        [(x * N_Y + (i + o) % N_Y, x * N_Y + i) for x in range(2) for i in range(N_Y)],
    )


def from_x(block):
    return lax.ppermute(block, "tensor", [(i, (i + N_Y) % (2 * N_Y)) for i in range(2 * N_Y)])


def dot_nt(a, b):
    return lax.dot_general(a, b, (((1,), (1,)), ((), ())), preferred_element_type=F32)


def dot_nn(a, b):
    return lax.dot_general(a, b, (((1,), (0,)), ((), ())), preferred_element_type=F32)


def call(kernel, grid, in_specs, out_specs, out_shape, flops=0, bytes_accessed=0, name=None):
    return pl.pallas_call(
        kernel,
        grid_spec=pltpu.PrefetchScalarGridSpec(
            num_scalar_prefetch=1, grid=grid, in_specs=in_specs, out_specs=out_specs
        ),
        out_shape=out_shape,
        name=name,
        compiler_params=pltpu.CompilerParams(vmem_limit_bytes=VMEM_BYTES),
        cost_estimate=pl.CostEstimate(
            flops=flops, bytes_accessed=bytes_accessed, transcendentals=0
        ),
    )


WHOLE = pl.BlockSpec(memory_space=pltpu.VMEM)


def normalize(place, hidden, gain):
    rows, width = hidden.shape
    part = width // N_Z

    def kernel(at_ref, h_ref, g_ref, r_ref, *out_refs):
        x = h_ref[...].astype(F32)
        r = lax.rsqrt(jnp.mean(x * x, axis=-1, keepdims=True) + 1e-06)
        r_ref[...] = jnp.broadcast_to(r, r_ref.shape)
        for d in range(N_Z):
            at = pl.multiple_of(lax.rem(at_ref[0] + d, N_Z) * part, part)
            x = h_ref[:, pl.ds(at, part)].astype(F32)
            g = g_ref[:, pl.ds(at, part)].astype(F32)
            out_refs[d][...] = ((x * r) * g).T.astype(BF16)

    return call(
        kernel,
        (),
        [WHOLE, WHOLE],
        [WHOLE] * (1 + N_Z),
        [jax.ShapeDtypeStruct((rows, 128), F32)]
        + [jax.ShapeDtypeStruct((part, rows), BF16)] * N_Z,
        bytes_accessed=4 * rows * width,
        name="normalize",
    )(place, hidden, gain)


def partial_sums(place, seqs, groups, g_own, g_par, w_own, w_par, extras=(), per_sequence=False):
    _, _, rows, cols = g_own.shape
    part = w_own.shape[0]
    half = part // 2
    step = 256
    steps = half // step
    count = len(seqs)
    jobs = [job for group in groups for job in group]
    qs = sorted({q for q, _, _ in jobs})
    sides = sorted({side for _, side, _ in jobs})
    n_g, n_w, n_e = 2 * count * len(qs), 2 * len(sides), len(extras)

    def kernel(at_ref, *refs):
        g_refs, w_refs = refs[:n_g], refs[n_g : n_g + n_w]
        e_refs, outs = refs[n_g + n_w : n_g + n_w + n_e], refs[n_g + n_w + n_e :]
        for k, group in enumerate(groups):
            for j, (q, side, adds) in enumerate(group):
                at = qs.index(q) * 2 * count
                left = jnp.concatenate([g_refs[at + o][0, 0] for o in range(count)], 0)
                right = jnp.concatenate([g_refs[at + count + o][0, 0] for o in range(count)], 0)
                s = sides.index(side) * 2
                total = dot_nt(left, w_refs[s][...]) + dot_nt(right, w_refs[s + 1][...])
                total = total.reshape(count, rows, step)
                for e, i in adds:
                    total = total + e_refs[e][i].astype(F32)
                if per_sequence:
                    for o in range(count):
                        outs[o][side] = total[o].astype(BF16)
                else:
                    outs[k][j] = total.astype(BF16)

    def tokens_of(o, q):
        return pl.BlockSpec(
            (1, 1, rows, cols),
            lambda i, at: (lax.rem(at[0] + o, N_Z), lax.rem(at[1] + q, N_Y), 0, 0),
        )

    def features_of(side):
        return pl.BlockSpec((step, cols), lambda i, at: (side * steps + i, 0))

    def chunk(n):
        return pl.BlockSpec((n, count, rows, step), lambda i, at: (0, 0, 0, i))

    in_specs, operands = [], []
    for q in qs:
        for array in (g_own, g_par):
            for o in seqs:
                in_specs.append(tokens_of(o, q))
                operands.append(array)
    for side in sides:
        for w in (w_own, w_par):
            in_specs.append(features_of(side))
            operands.append(w)
    in_specs += [chunk(e.shape[0]) for e in extras]
    operands += list(extras)
    if per_sequence:
        out_specs = [pl.BlockSpec((2, rows, step), lambda i, at: (0, 0, i))] * count
        out_shape = [jax.ShapeDtypeStruct((2, rows, half), BF16)] * count
    else:
        out_specs = [chunk(len(group)) for group in groups]
        out_shape = [
            jax.ShapeDtypeStruct((len(group), count, rows, half), BF16) for group in groups
        ]
    return call(
        kernel, (steps,), in_specs, out_specs, out_shape, name="partial_sums"
    )(place, *operands)


def weight_terms(place, n_pieces, g):
    part, rows = n_pieces[0][0].shape
    cols = g.shape[3]
    step = 512

    def kernel(at_ref, *refs):
        n_refs, (g_ref, out_ref) = refs[: N_Z * N_Y], refs[N_Z * N_Y :]
        total = None
        for o in range(N_Z):
            left = jnp.concatenate([n_refs[o * N_Y + q][...] for q in range(N_Y)], 1)
            z = lax.rem(at_ref[0] + o, N_Z)
            right = jnp.concatenate(
                [g_ref[z, lax.rem(at_ref[1] + q, N_Y)] for q in range(N_Y)], 0
            )
            term = dot_nn(left, right)
            total = term if total is None else total + term
        out_ref[...] = total.astype(BF16)

    return call(
        kernel,
        (part // step,),
        [pl.BlockSpec((step, rows), lambda i, at: (i, 0))] * (N_Z * N_Y)
        + [pl.BlockSpec((N_Z, N_Y, rows, cols), lambda i, at: (0, 0, 0, 0))],
        pl.BlockSpec((step, cols), lambda i, at: (i, 0)),
        jax.ShapeDtypeStruct((part, cols), BF16),
        name="weight_terms",
    )(place, *[n_pieces[o][q] for o in range(N_Z) for q in range(N_Y)], g)


def finish(place, deviation, gain, hidden, received, h):
    rows, width = hidden.shape
    part = width // N_Z
    half = part // 2
    step = 32

    def kernel(at_ref, r_ref, g_ref, x_ref, u_ref, *refs):
        h_refs, out_ref = refs[:-1], refs[-1]
        r = r_ref[:, :1]
        spots = [
            (o, s, pl.multiple_of(lax.rem(at_ref[0] + o, N_Z) * part + s * half, half))
            for o in range(N_Z)
            for s in range(2)
        ]

        def terms(o, s, at):
            xhat = x_ref[:, pl.ds(at, half)].astype(F32) * r
            scaled = g_ref[:, pl.ds(at, half)].astype(F32) * h_refs[o][s].astype(F32)
            return xhat, scaled

        total = jnp.zeros((step, 1), F32)
        for spot in spots:
            xhat, scaled = terms(*spot)
            total += jnp.sum(scaled * xhat, axis=-1, keepdims=True)
        mean = total / width
        for spot in spots:
            xhat, scaled = terms(*spot)
            at = spot[2]
            up = u_ref[0, :, pl.ds(at, half)].astype(F32)
            out_ref[0, :, pl.ds(at, half)] = (up + r * (scaled - xhat * mean)).astype(BF16)

    return call(
        kernel,
        (rows // step,),
        [
            pl.BlockSpec((step, 128), lambda i, at: (i, 0)),
            pl.BlockSpec((1, width), lambda i, at: (0, 0)),
            pl.BlockSpec((step, width), lambda i, at: (i, 0)),
            pl.BlockSpec((1, step, width), lambda i, at: (0, i, 0)),
        ]
        + [pl.BlockSpec((2, step, half), lambda i, at: (0, i, 0))] * N_Z,
        pl.BlockSpec((1, step, width), lambda i, at: (0, i, 0)),
        jax.ShapeDtypeStruct((1, rows, width), BF16),
        name="finish",
    )(place, deviation, gain, hidden, received, *h)


def shards(hidden_in, norm_gain, qkv_weight, qkv_grad, upper_grad):
    tensor = lax.axis_index("tensor")
    xh, y, z = tensor // N_Y, tensor % N_Y, lax.axis_index("dp")
    place = jnp.stack([z, y]).astype(jnp.int32)
    rows = hidden_in.shape[1]
    part = hidden_in.shape[2] // N_Z
    cols = qkv_grad.shape[2]
    layers = lax.axis_size("pipe")
    chains = Chains()

    def yy(block, o, depth=1):
        return chains("y%d" % o, block, lambda b: from_y(b, o), depth)

    def xx(block):
        return chains("x", block, from_x)

    grads = qkv_grad[0].reshape(2, N_Y, rows, cols)
    par0 = xx(lax.dynamic_index_in_dim(grads, 1 - xh, 0, keepdims=False))
    g_own = lax.all_gather(lax.dynamic_index_in_dim(grads, xh, 0, keepdims=False), "dp")

    deviation, *n_to = normalize(place, hidden_in[0], norm_gain)
    n1, n3 = from_z(n_to[3], 1), from_z(n_to[1], 3)
    n_up, n_down = {0: yy(n_to[0], 1, 2)}, {0: yy(n_to[0], 3, 2)}
    n2 = from_z(after(n_to[2], n1, n3), 2)
    n_near = [n_to[0], n1, n2, n3]

    g_par = lax.all_gather(after(par0, n1, n3), "dp")
    w_own = lax.dynamic_slice_in_dim(qkv_weight[0], z * part, part, 0)
    w_par = xx(after(w_own, n1, n3, n_up[0], n_down[0]))
    received = lax.ppermute(
        after(upper_grad, w_par), "pipe", [(i + 1, i) for i in range(layers - 1)]
    )
    for o in (1, 3, 2):
        n_up[o], n_down[o] = yy(n_near[o], 1, 2), yy(n_near[o], 3, 2)
    n_across = {}
    for one, other in ((0, 1), (3, 2)):
        n_across[one], n_across[other] = yy(n_up[one], 1, 2), yy(n_down[other], 3, 2)
    n_pieces = [[n_near[o], n_up[o], n_across[o], n_down[o]] for o in range(N_Z)]

    dw_got = xx(weight_terms(place, n_pieces, g_par))
    dw_own = weight_terms(place, n_pieces, g_own)

    sums = functools.partial(partial_sums, place, g_own=g_own, g_par=g_par, w_own=w_own, w_par=w_par)

    def first(seqs):
        up, down = sums(seqs, [[(2, 0, ()), (1, 1, ())], [(2, 1, ()), (3, 0, ())]])
        return yy(up, 3), yy(down, 1)

    def second(seqs, up, down):
        up2, down2 = sums(seqs, [[(1, 0, [(0, 0)])], [(3, 1, [(1, 0)])]], extras=[up, down])
        return yy(up2, 3), yy(down2, 1)

    def third(seqs, up, down, up2, down2):
        return sums(
            seqs,
            [[(0, 0, [(1, 1), (2, 0)]), (0, 1, [(0, 1), (3, 0)])]],
            extras=[up, down, up2, down2],
            per_sequence=True,
        )

    here, there = [2, 3], [1, 0]
    one = first(here)
    two = first(there)
    one = one + second(here, after(one[0], received), one[1])
    two = two + second(there, *two)
    h_to2, h_to3 = third(here, after(one[0], dw_own), *one[1:])
    h2, h1 = from_z(h_to2, 2), from_z(h_to3, 1)
    h_to1, h0 = third(there, *two)
    h3 = from_z(h_to1, 3)

    weight_out = (dw_own.astype(F32) + after(dw_got, h1, h2).astype(F32)).astype(BF16)
    input_out = finish(place, deviation, norm_gain, hidden_in[0], received, [h0, h1, h2, h3])
    return (weight_out[None], input_out)


def solution(mesh):
    placed = (
        P("pipe", ("dp", "tensor"), None),
        P("pipe", None),
        P("pipe", None, "tensor"),
        P("pipe", "dp", "tensor"),
        P("pipe", ("dp", "tensor"), None),
    )
    return jax.shard_map(
        shards,
        mesh=mesh,
        in_specs=placed,
        out_specs=(P("pipe", "dp", "tensor"), P("pipe", ("dp", "tensor"), None)),
        check_vma=False,
    )
```

```python
import functools

import jax
import jax.numpy as jnp
from jax import lax
from jax.experimental import pallas as pl
from jax.experimental.pallas import tpu as pltpu
from jax.sharding import PartitionSpec as P

N_Z = 4
N_Y = 4
F32 = jnp.float32
BF16 = jnp.bfloat16
VMEM_BYTES = 20 * 2**20


class Chains:
    def __init__(self):
        self.last = {}

    def __call__(self, key, block, send):
        if key in self.last:
            block = after(block, self.last[key])
        return self.hold(key, send(block))

    def hold(self, *keys_and_sent):
        for key in keys_and_sent[:-1]:
            self.last[key] = keys_and_sent[-1]
        return keys_and_sent[-1]


def after(block, *others):
    return lax.optimization_barrier((block, *others))[0]


def from_z(block, o):
    return lax.ppermute(block, "dp", [((i + o) % N_Z, i) for i in range(N_Z)])


def from_y(block, o):
    return lax.ppermute(
        block,
        "tensor",
        [(x * N_Y + (i + o) % N_Y, x * N_Y + i) for x in range(2) for i in range(N_Y)],
    )


def from_x(block):
    return lax.ppermute(block, "tensor", [(i, (i + N_Y) % (2 * N_Y)) for i in range(2 * N_Y)])


def dot_nt(a, b):
    return lax.dot_general(a, b, (((1,), (1,)), ((), ())), preferred_element_type=F32)


def dot_nn(a, b):
    return lax.dot_general(a, b, (((1,), (0,)), ((), ())), preferred_element_type=F32)


def call(kernel, grid, in_specs, out_specs, out_shape, flops=0, bytes_accessed=0, name=None):
    return pl.pallas_call(
        kernel,
        grid_spec=pltpu.PrefetchScalarGridSpec(
            num_scalar_prefetch=1, grid=grid, in_specs=in_specs, out_specs=out_specs
        ),
        out_shape=out_shape,
        name=name,
        compiler_params=pltpu.CompilerParams(vmem_limit_bytes=VMEM_BYTES),
        cost_estimate=pl.CostEstimate(
            flops=flops, bytes_accessed=bytes_accessed, transcendentals=0
        ),
    )


WHOLE = pl.BlockSpec(memory_space=pltpu.VMEM)


def normalize(place, hidden, gain):
    rows, width = hidden.shape
    part = width // N_Z

    def kernel(at_ref, h_ref, g_ref, r_ref, *out_refs):
        x = h_ref[...].astype(F32)
        r = lax.rsqrt(jnp.mean(x * x, axis=-1, keepdims=True) + 1e-06)
        r_ref[...] = jnp.broadcast_to(r, r_ref.shape)
        for d in range(N_Z):
            at = pl.multiple_of(lax.rem(at_ref[0] + d, N_Z) * part, part)
            x = h_ref[:, pl.ds(at, part)].astype(F32)
            g = g_ref[:, pl.ds(at, part)].astype(F32)
            out_refs[d][0] = ((x * r) * g).T.astype(BF16)

    return call(
        kernel,
        (),
        [WHOLE, WHOLE],
        [WHOLE] * (1 + N_Z),
        [jax.ShapeDtypeStruct((rows, 128), F32)]
        + [jax.ShapeDtypeStruct((1, part, rows), BF16)] * N_Z,
        bytes_accessed=4 * rows * width,
        name="normalize",
    )(place, hidden, gain)


def partial_sums(place, seqs, groups, g_own, g_par, w_own, w_par, extras=(), per_sequence=False):
    _, _, rows, cols = g_own[0][0].shape
    part = w_own.shape[0]
    half = part // 2
    step = 256
    steps = half // step
    count = len(seqs)
    jobs = [job for group in groups for job in group]
    qs = sorted({q for q, _, _ in jobs})
    sides = sorted({side for _, side, _ in jobs})
    n_g, n_w, n_e = 2 * count * len(qs), 2 * len(sides), len(extras)

    def kernel(at_ref, *refs):
        g_refs, w_refs = refs[:n_g], refs[n_g : n_g + n_w]
        e_refs, outs = refs[n_g + n_w : n_g + n_w + n_e], refs[n_g + n_w + n_e :]
        for k, group in enumerate(groups):
            for j, (q, side, adds) in enumerate(group):
                at = qs.index(q) * 2 * count
                left = jnp.concatenate([g_refs[at + o][0, 0] for o in range(count)], 0)
                right = jnp.concatenate([g_refs[at + count + o][0, 0] for o in range(count)], 0)
                s = sides.index(side) * 2
                total = dot_nt(left, w_refs[s][...]) + dot_nt(right, w_refs[s + 1][...])
                total = total.reshape(count, rows, step)
                for e, i in adds:
                    total = total + e_refs[e][i * count : (i + 1) * count].astype(F32)
                if per_sequence:
                    for o in range(count):
                        outs[o][side] = total[o].astype(BF16)
                else:
                    outs[k][j * count : (j + 1) * count] = total.astype(BF16)

    def tokens_of(index, q):
        return pl.BlockSpec(
            (1, 1, rows, cols), lambda i, at: (index, lax.rem(at[1] + q, N_Y), 0, 0)
        )

    def features_of(side):
        return pl.BlockSpec((step, cols), lambda i, at: (side * steps + i, 0))

    def chunk(n):
        return pl.BlockSpec((n, rows, step), lambda i, at: (0, 0, i))

    in_specs, operands = [], []
    for q in qs:
        for g in (g_own, g_par):
            for o in seqs:
                in_specs.append(tokens_of(g[o][1], q))
                operands.append(g[o][0])
    for side in sides:
        for w in (w_own, w_par):
            in_specs.append(features_of(side))
            operands.append(w)
    in_specs += [chunk(e.shape[0]) for e in extras]
    operands += list(extras)
    if per_sequence:
        out_specs = [pl.BlockSpec((2, rows, step), lambda i, at: (0, 0, i))] * count
        out_shape = [jax.ShapeDtypeStruct((2, rows, half), BF16)] * count
    else:
        out_specs = [chunk(len(group) * count) for group in groups]
        out_shape = [
            jax.ShapeDtypeStruct((len(group) * count, rows, half), BF16) for group in groups
        ]
    return call(
        kernel, (steps,), in_specs, out_specs, out_shape, name="partial_sums"
    )(place, *operands)


def weight_terms(place, n_pieces, g):
    _, part, rows = n_pieces[0][0][0].shape
    cols = g[0][0].shape[3]
    step = 256

    def kernel(at_ref, *refs):
        n_refs, g_refs, out_ref = refs[: N_Z * N_Y], refs[N_Z * N_Y : -1], refs[-1]
        total = None
        for o in range(N_Z):
            left = jnp.concatenate([n_refs[o * N_Y + q][0] for q in range(N_Y)], 1)
            right = jnp.concatenate(
                [g_refs[o][0, lax.rem(at_ref[1] + q, N_Y)] for q in range(N_Y)], 0
            )
            term = dot_nn(left, right)
            total = term if total is None else total + term
        out_ref[...] = total.astype(BF16)

    def piece(index):
        return pl.BlockSpec((1, step, rows), lambda i, at: (index, i, 0))

    def tokens(index):
        return pl.BlockSpec((1, N_Y, rows, cols), lambda i, at: (index, 0, 0, 0))

    flat = [n_pieces[o][q] for o in range(N_Z) for q in range(N_Y)]
    return call(
        kernel,
        (part // step,),
        [piece(index) for _, index in flat] + [tokens(index) for _, index in g],
        pl.BlockSpec((step, cols), lambda i, at: (i, 0)),
        jax.ShapeDtypeStruct((part, cols), BF16),
        name="weight_terms",
    )(place, *[array for array, _ in flat], *[array for array, _ in g])


def finish(place, deviation, gain, hidden, received, h):
    rows, width = hidden.shape
    part = width // N_Z
    half = part // 2
    step = 32

    def kernel(at_ref, r_ref, g_ref, x_ref, u_ref, *refs):
        h_refs, out_ref = refs[:-1], refs[-1]
        r = r_ref[:, :1]
        spots = [
            (o, s, pl.multiple_of(lax.rem(at_ref[0] + o, N_Z) * part + s * half, half))
            for o in range(N_Z)
            for s in range(2)
        ]

        def terms(o, s, at):
            xhat = x_ref[:, pl.ds(at, half)].astype(F32) * r
            scaled = g_ref[:, pl.ds(at, half)].astype(F32) * h_refs[o][s].astype(F32)
            return xhat, scaled

        total = jnp.zeros((step, 1), F32)
        for spot in spots:
            xhat, scaled = terms(*spot)
            total += jnp.sum(scaled * xhat, axis=-1, keepdims=True)
        mean = total / width
        for spot in spots:
            xhat, scaled = terms(*spot)
            at = spot[2]
            up = u_ref[0, :, pl.ds(at, half)].astype(F32)
            out_ref[0, :, pl.ds(at, half)] = (up + r * (scaled - xhat * mean)).astype(BF16)

    return call(
        kernel,
        (rows // step,),
        [
            pl.BlockSpec((step, 128), lambda i, at: (i, 0)),
            pl.BlockSpec((1, width), lambda i, at: (0, 0)),
            pl.BlockSpec((step, width), lambda i, at: (i, 0)),
            pl.BlockSpec((1, step, width), lambda i, at: (0, i, 0)),
        ]
        + [pl.BlockSpec((2, step, half), lambda i, at: (0, i, 0))] * N_Z,
        pl.BlockSpec((1, step, width), lambda i, at: (0, i, 0)),
        jax.ShapeDtypeStruct((1, rows, width), BF16),
        name="finish",
    )(place, deviation, gain, hidden, received, *h)


def shards(hidden_in, norm_gain, qkv_weight, qkv_grad, upper_grad):
    tensor = lax.axis_index("tensor")
    xh, y, z = tensor // N_Y, tensor % N_Y, lax.axis_index("dp")
    place = jnp.stack([z, y]).astype(jnp.int32)
    rows = hidden_in.shape[1]
    part = hidden_in.shape[2] // N_Z
    cols = qkv_grad.shape[2]
    layers = lax.axis_size("pipe")
    chains = Chains()

    def zz(block, o):
        return chains("z%d" % o, block, lambda b: from_z(b, o))

    def yy(block, o):
        return chains("y%d" % o, block, lambda b: from_y(b, o))

    def xx(block):
        return chains("x", block, from_x)

    grads = qkv_grad[0].reshape(2, N_Y, rows, cols)
    par0 = xx(lax.dynamic_slice_in_dim(grads, 1 - xh, 1, 0))

    deviation, *n_to = normalize(place, hidden_in[0], norm_gain)
    n1, n3 = zz(n_to[3], 1), zz(n_to[1], 3)
    n2 = chains.hold("z1", "z3", from_z(after(n_to[2], n1, n3), 2))
    w_own = lax.dynamic_slice_in_dim(qkv_weight[0], z * part, part, 0)
    n_near = [after(n_to[0], w_own), n1, n2, n3]
    n_up, n_down, n_across = {}, {}, {}
    for o in (0, 1, 3, 2):
        n_up[o], n_down[o] = yy(n_near[o], 1), yy(n_near[o], 3)
    for one, other in ((0, 1), (3, 2)):
        n_across[one], n_across[other] = yy(n_up[one], 1), yy(n_down[other], 3)
    n_pieces = [
        [(n_near[o], 0), (n_up[o], 0), (n_across[o], 0), (n_down[o], 0)] for o in range(N_Z)
    ]

    own0 = lax.dynamic_slice_in_dim(grads, xh, 1, 0)
    own1, own3 = zz(own0, 1), zz(own0, 3)
    par1, par3 = zz(par0, 1), zz(par0, 3)
    own2, par2 = zz(own1, 1), zz(par3, 3)
    g_own = [(own0, 0), (own1, 0), (own2, 0), (own3, 0)]
    g_par = [(par0, 0), (par1, 0), (par2, 0), (par3, 0)]

    w_par = xx(w_own)
    moved = (n_near, n_up, n_down, n_across, own0, own1, own2, own3, par0, par1, par2, par3)
    moved, w_own, w_par, upper_grad = lax.optimization_barrier((moved, w_own, w_par, upper_grad))
    n_near, n_up, n_down, n_across, own0, own1, own2, own3, par0, par1, par2, par3 = moved
    n_pieces = [
        [(n_near[o], 0), (n_up[o], 0), (n_across[o], 0), (n_down[o], 0)] for o in range(N_Z)
    ]
    g_own = [(own0, 0), (own1, 0), (own2, 0), (own3, 0)]
    g_par = [(par0, 0), (par1, 0), (par2, 0), (par3, 0)]

    dw_partner = weight_terms(place, n_pieces, g_par)
    dw_got = xx(dw_partner)

    sums = functools.partial(partial_sums, place, g_own=g_own, g_par=g_par, w_own=w_own, w_par=w_par)
    far = [1, 2, 3]
    p2a, p2b = sums(far, [[(2, 0, ())], [(2, 1, ())]])
    hop_up, hop_down = yy(p2a, 3), yy(p2b, 1)
    dw_own = weight_terms(place, n_pieces, g_own)
    p1b, p3a = sums(far, [[(1, 1, ())], [(3, 0, ())]], w_par=after(w_par, dw_partner))
    up_b, down_a = yy(p1b, 3), yy(p3a, 1)
    p1a, p3b = sums(
        far,
        [[(1, 0, [(0, 0)])], [(3, 1, [(1, 0)])]],
        extras=[hop_up, hop_down],
    )
    up_a, down_b = yy(p1a, 3), yy(p3b, 1)
    up, down = sums([0], [[(2, 0, ()), (1, 1, ())], [(2, 1, ()), (3, 0, ())]])
    h_to1, h_to2, h_to3 = sums(
        far,
        [[(0, 0, [(0, 0), (1, 0)]), (0, 1, [(2, 0), (3, 0)])]],
        extras=[after(up_a, dw_own, up), down_a, down_b, up_b],
        per_sequence=True,
    )
    received = lax.ppermute(after(upper_grad, p1a), "pipe", [(i + 1, i) for i in range(layers - 1)])
    h2 = from_z(h_to2, 2)
    h1, h3 = from_z(after(h_to3, h2), 1), from_z(after(h_to1, h2), 3)

    up, down = yy(after(up, h_to2), 3), yy(after(down, h_to2), 1)
    p1a, p3b = sums([0], [[(1, 0, [(0, 0)])], [(3, 1, [(1, 0)])]], extras=[after(up, h2), down])
    up2, down2 = yy(p1a, 3), yy(p3b, 1)
    (h0,) = sums(
        [0],
        [[(0, 0, [(1, 1), (2, 0)]), (0, 1, [(0, 1), (3, 0)])]],
        extras=[after(up, h1, h3), down, up2, down2],
        per_sequence=True,
    )

    weight_out = (dw_own.astype(F32) + dw_got.astype(F32)).astype(BF16)
    input_out = finish(place, deviation, norm_gain, hidden_in[0], received, [h0, h1, h2, h3])
    return (weight_out[None], input_out)


def solution(mesh):
    placed = (
        P("pipe", ("dp", "tensor"), None),
        P("pipe", None),
        P("pipe", None, "tensor"),
        P("pipe", "dp", "tensor"),
        P("pipe", ("dp", "tensor"), None),
    )
    return jax.shard_map(
        shards,
        mesh=mesh,
        in_specs=placed,
        out_specs=(P("pipe", "dp", "tensor"), P("pipe", ("dp", "tensor"), None)),
        check_vma=False,
    )
```
